32 devices in a mesh: lat: 4 (over y, core), lon: 8 (over z, x).
Axes of the slice: x: 2, y: 2, z: 4, core: 2. Of those that a mesh axis runs over, the one named last changes fastest.
Arguments:
- depth: float32 [32, 8192], P('lat', 'lon'), may hold values from 0.5 to 4
- friction: float32 [32, 8192], P('lat', 'lon'), may hold values from 0.2 to 2
- ocean_mask: int32 [32, 8192], P('lat', 'lon'), may hold values 0 or 1
- forcing: float32 [16, 32, 8192], P(None, 'lat', 'lon'), may hold values from -24 to 24
- tile_route: int32 [512, 1], P(('lat', 'lon')), may hold values from 0 to 7; in each aligned block of 16 rows (0 to 15, 16 to 31, ...) at most 2 rows name the same one
- tile_block: int32 [512], P(('lat', 'lon')), may hold values from 0 to 63
- obs_cell: int32 [512, 128], P(('lat', 'lon')), may hold values from 0 to 127
- obs_time: float32 [512, 128], P(('lat', 'lon')), may hold values from 0 to 720
- obs_value: float32 [512, 128], P(('lat', 'lon')), may hold values from -6 to 6
- obs_weight: float32 [512, 128], P(('lat', 'lon')), may hold values from 0.5 to 4
Outputs:
- elevation: float32 [16, 32, 8192], P(None, 'lat', 'lon')
- residual: float32 [16, 32, 8192], P(None, 'lat', 'lon')
The draws below stay inside these ranges and needn't reach their ends.
Inputs may be any that keep to these rules, and one draw needn't show every extreme that they name: `tile_route`: among the 16 tiles of one device at most 2 name the same owner, and in some device exactly 2 do.
All inputs are finite; a program needn't handle non-finite values. No bound on the sum of `ocean_mask` on one device may be relied on, other than what follows from the above.
Results may differ from the reference program's by a relative error of at most 0.0007.
Values sent between devices are 32-bit elements; how exact they have to be, the bound alone decides.
A program may use at most 64 MiB of HBM per device.

```python
import math
import jax
import jax.numpy as jnp
import numpy as np
from jax import lax

NC = 8
CLAT = 8
CLON = 1024
TILES_DEV = 16
OBS_TILE = 128
BLOCK = 128
CAP = 2
ITERS = 3
OUTER = 2
CHANNELS = 16
NLAT = 32
NLON = 8192
OWNERS = 8
NTILES = 512
BLOCKS_DEV = 64
N_LON = 8


def draw_forcing(key, part):
    first_key, second_key = jax.random.split(jax.random.fold_in(key, 11))
    latitude = jnp.arange(NLAT, dtype=jnp.float32) / max(NLAT - 1, 1)
    jitter = jnp.exp(jax.random.uniform(second_key, (1, NLAT, 1), minval=-0.35, maxval=0.35))
    base = jnp.clip(jax.random.normal(first_key, (2 * NC, NLAT, NLON)), -5.0, 5.0)
    envelope = 3.0 ** latitude
    return (base * envelope[None, :, None] * jitter).astype(jnp.float32)


def place_ends(result, own_key, least, top_value):
    extent = result.shape
    place = [jax.random.randint(jax.random.fold_in(own_key, axis), (), 0, extent[axis]) for axis in range(len(extent))]
    result = result.at[tuple(place)].set(least)
    longest = extent.index(max(extent))
    place[longest] = (place[longest] + 1) % extent[longest]
    return result.at[tuple(place)].set(top_value)


def steps_of(own_key, extent, pieces, low, largest):
    level, own = 1.0, jax.random.fold_in(own_key, 6)
    for dim, blocks in pieces:
        steps = jnp.exp(jax.random.uniform(jax.random.fold_in(own, dim), (blocks,), jnp.float32, low / len(pieces), largest / len(pieces)))
        level = level * jnp.repeat(steps, extent[dim] // blocks).reshape([-1 if axis == dim else 1 for axis in range(len(extent))])
    return level


def assign_block(rng, own, number, rows, number_of, top, most, lean):
    order = jax.random.permutation(rng, number_of)
    packed, common = portions_of(number_of, rows * top, most, lean, True), portions_of(number_of, rows * top, most, lean, False)
    places = jnp.arange(number_of)

    def named(lengths, turn):
        used = int((lengths > 0).sum())
        fixed = max(1, used // 4)
        moved = fixed + (places - fixed + turn * (used - fixed)) % max(1, number_of - fixed)
        return jnp.zeros((number_of,), jnp.int32).at[order[jnp.where(places < fixed, places, moved)]].set(jnp.asarray(lengths, jnp.int32))

    lengths = jnp.where(number % 4 == 0, named(packed, number // 4), named(common, number - number // 4 - 1))
    mixed = jax.random.permutation(jax.random.fold_in(own, 3), number_of)
    source_of, sink = mixed[0:number_of // 2 * 2:2], mixed[1:number_of // 2 * 2:2]
    room = jnp.minimum(lengths[source_of] - 1, most - lengths[sink]) // 2
    room = jnp.where((source_of == order[0]) | (sink == order[0]) | (lengths[sink] == 0), 0, jnp.maximum(room, 0))
    moved = jax.random.randint(jax.random.fold_in(own, 4), (number_of // 2,), 0, 1 << 20) % (room + 1)
    lengths = lengths.at[source_of].add(-moved).at[sink].add(moved)
    items = jnp.searchsorted(jnp.cumsum(lengths), jnp.arange(rows * top), side="right").astype(jnp.int32)
    listing = items.reshape(top, rows).T
    listing = listing[jax.random.permutation(jax.random.fold_in(own, 1), rows)]
    turn = jax.random.randint(jax.random.fold_in(own, 2), (rows, 1), 0, top)
    return jnp.take_along_axis(listing, (jnp.arange(top)[None, :] + turn) % top, axis=1)


def portions_of(amount, total, reach, slope, full):
    loads = [(1 << 20) // math.isqrt(rank ** slope) + 1 for rank in range(1, amount + 1)]
    largest = reach if full else min(reach, max(-(-total // amount), total * loads[0] // sum(loads)))
    least = 1 if total - largest >= amount - 1 else 0
    holding, spare = [largest] + [least] * (amount - 1), total - largest - least * (amount - 1)
    while spare > 0:
        candidates = [i for i in range(1, amount) if holding[i] < largest] or [i for i in range(1, amount) if holding[i] < reach]
        pool, left = sum([loads[i] for i in candidates]), spare
        for i in candidates:
            addition = min(reach - holding[i], max(1, left * loads[i] // pool), spare)
            holding[i] = holding[i] + addition
            spare = spare - addition
    return np.array(holding)


def noise(key, shape, width, most, shards=(), kind=jnp.bfloat16):
    result = width * jax.random.normal(key, shape, jnp.float32)
    if shards:
        result = result * steps_of(key, shape, shards, -0.22, 0.18)
    return jnp.clip(result, -most, most).astype(kind)


def setup_inputs(seed: int = 0) -> dict:
    seeds = jax.random.split(jax.random.key(seed), 11)
    depth = jnp.clip(jnp.exp(math.log(4.0) - 2.0794415 * jax.random.uniform(seeds[0], (NLAT, NLON), jnp.float32) ** steps_of(seeds[0], (NLAT, NLON), ((0, 4), (1, 8)), -0.2, 0.2)), 0.5, 4.0)
    friction = jnp.clip(jnp.exp(math.log(2.0) - 2.3025851 * jax.random.uniform(seeds[1], (NLAT, NLON), jnp.float32) ** steps_of(seeds[1], (NLAT, NLON), ((0, 4), (1, 8)), -0.2, 0.2)), 0.2, 2.0)
    ocean_mask = place_ends((jax.random.randint(seeds[2], (NLAT, NLON), 0, 4) < 3).astype(jnp.int32), jax.random.fold_in(seeds[2], 1), 0, 1)
    forcing = draw_forcing(jax.random.fold_in(seeds[10], 71), 0)
    tile_route_keys = jax.random.split(jax.random.fold_in(seeds[4], 1), NTILES // TILES_DEV)
    tile_route_turns = jax.random.permutation(jax.random.fold_in(seeds[4], 3), NTILES // TILES_DEV)
    tile_route = jax.vmap(lambda own, number: assign_block(jax.random.fold_in(seeds[4], 2), own, number, TILES_DEV, OWNERS, 1, CAP, 2))(tile_route_keys, tile_route_turns).reshape((NTILES, 1))
    tile_block = place_ends(jax.random.randint(seeds[5], (NTILES,), 0, BLOCKS_DEV), jax.random.fold_in(seeds[5], 1), 0, BLOCKS_DEV - 1).astype(jnp.int32)
    obs_cell = place_ends(jax.random.randint(seeds[6], (NTILES, OBS_TILE), 0, BLOCK), jax.random.fold_in(seeds[6], 1), 0, BLOCK - 1).astype(jnp.int32)
    obs_time = jnp.clip(720.0 * jax.random.uniform(seeds[7], (NTILES, OBS_TILE), jnp.float32) ** steps_of(seeds[7], (NTILES, OBS_TILE), ((0, 32),), -0.2, 0.2), 0.0, 720.0)
    obs_value = noise(seeds[8], (NTILES, OBS_TILE), 1.0, 6.0, ((0, 32),), jnp.float32)
    obs_weight = jnp.clip(jnp.exp(math.log(4.0) - 2.0794415 * jax.random.uniform(seeds[9], (NTILES, OBS_TILE), jnp.float32) ** steps_of(seeds[9], (NTILES, OBS_TILE), ((0, 32),), -0.2, 0.2)), 0.5, 4.0)
    return {"depth": depth, "friction": friction, "ocean_mask": ocean_mask, "forcing": forcing, "tile_route": tile_route, "tile_block": tile_block, "obs_cell": obs_cell, "obs_time": obs_time, "obs_value": obs_value, "obs_weight": obs_weight}


OMEGA_DEGREES = (28.984104, 30.0, 28.43973, 30.082137, 15.041069, 13.943036, 14.958931, 13.398661)

def angular_rates():
    return jnp.array(OMEGA_DEGREES, dtype=jnp.float32) * (math.pi / 180.0)

def harmonic(first, second):
    return 2.0 * first * second / (first + second)

def neighbours(vector):
    east = jnp.roll(vector, -1, axis=2)
    west = jnp.roll(vector, 1, axis=2)
    north = jnp.concatenate([vector[:, 1:], jnp.zeros_like(vector[:, :1])], axis=1)
    south = jnp.concatenate([jnp.zeros_like(vector[:, :1]), vector[:, :-1]], axis=1)
    return (east, west, north, south)

def reference(depth, friction, ocean_mask, forcing, tile_route, tile_block, obs_cell, obs_time, obs_value, obs_weight):
    wet = ocean_mask.astype(jnp.float32)
    depth_east = jnp.roll(depth, -1, axis=1)
    wet_east = jnp.roll(wet, -1, axis=1)
    east_coef = wet * wet_east * harmonic(depth, depth_east)
    depth_north = jnp.concatenate([depth[1:], depth[:1]], axis=0)
    wet_north = jnp.concatenate([wet[1:], jnp.zeros_like(wet[:1])], axis=0)
    north_coef = wet * wet_north * harmonic(depth, depth_north)
    west_coef = jnp.roll(east_coef, 1, axis=1)
    south_coef = jnp.concatenate([jnp.zeros_like(north_coef[:1]), north_coef[:-1]], axis=0)
    rates = angular_rates()
    stiff_half = 0.2 * (rates / rates[0]) ** 2
    stiffness = jnp.concatenate([stiff_half, stiff_half])
    tile_ids = jnp.arange(NTILES, dtype=jnp.int32)
    lat_device = tile_ids // TILES_DEV // N_LON
    per_row = CLON // BLOCK
    row_index = lat_device * CLAT + tile_block // per_row
    col_index = tile_route[:, 0][:, None] * CLON + (tile_block % per_row)[:, None] * BLOCK + obs_cell
    rows_flat = jnp.broadcast_to(row_index[:, None], obs_cell.shape).reshape(-1).astype(jnp.int32)
    cols_flat = col_index.reshape(-1).astype(jnp.int32)
    flat_times = obs_time.reshape(-1)
    angles = rates[:, None] * flat_times[None, :]
    basis = jnp.concatenate([jnp.cos(angles), jnp.sin(angles)], axis=0)
    weights = obs_weight.reshape(-1)

    def spread(contrib):
        return jnp.zeros((CHANNELS, NLAT, NLON), jnp.float32).at[:, rows_flat, cols_flat].add(contrib)

    def observe(vector):
        projected = lax.optimization_barrier(jnp.sum(basis * vector[:, rows_flat, cols_flat], axis=0))
        return spread(weights * projected * basis)
    rhs = wet * forcing + spread(weights * obs_value.reshape(-1) * basis)

    def apply_with(vector, diagonal, sides):
        east, west, north, south = sides
        return diagonal * vector + east_coef * (vector - east) + west_coef * (vector - west) + north_coef * (vector - north) + south_coef * (vector - south) + observe(vector)

    def operate(vector, diagonal):
        return apply_with(vector, diagonal, neighbours(vector))
    elevation = jnp.zeros((CHANNELS, NLAT, NLON), jnp.float32)
    residual = rhs
    for outer_turn in range(OUTER):
        sides = neighbours(elevation)
        east, west, north, south = sides
        east_flux = east_coef * (east - elevation)
        north_flux = north_coef * (north - elevation)
        speed_sq = lax.optimization_barrier(jnp.sum(east_flux * east_flux + north_flux * north_flux, axis=0))
        drag = friction * jnp.sqrt(1.0 + speed_sq / (2 * NC))
        diagonal = wet * (stiffness[:, None, None] + drag) + (1.0 - wet)
        residual = rhs - apply_with(elevation, diagonal, sides)
        direction = residual
        norm_now = jnp.sum(residual * residual)
        for turn in range(ITERS):
            image = operate(direction, diagonal)
            step_size = norm_now / jnp.sum(direction * image)
            elevation = elevation + step_size * direction
            residual = residual - step_size * image
            norm_next = jnp.sum(residual * residual)
            direction = residual + norm_next / norm_now * direction
            norm_now = norm_next
    return (elevation, residual)
```

```python
import functools
import math

import jax
import jax.numpy as jnp
import numpy as np
from jax import lax
from jax.experimental import pallas as pl
from jax.experimental.pallas import tpu as pltpu
from jax.sharding import PartitionSpec as P

BLOCK = 128
CAP = 2
ITERS = 3
OUTER = 2
STEPS = ITERS * OUTER
MESH = pl.DeviceIdType.MESH
OMEGA_DEGREES = (28.984104, 30.0, 28.43973, 30.082137, 15.041069, 13.943036, 14.958931, 13.398661)
RATES = np.array(OMEGA_DEGREES, np.float32) * np.float32(math.pi / 180.0)
STIFF = np.float32(0.2) * (RATES / RATES[0]) ** 2


def sin_cos(angle):
    turn = jnp.floor(angle * (2.0 / math.pi) + 0.5)
    x = ((angle - turn * 1.5703125) - turn * 4.837512969970703125e-4) - turn * 7.54978995489188216e-8
    z = x * x
    s = ((-1.9515295891e-4 * z + 8.3321608736e-3) * z - 1.6666654611e-1) * z * x + x
    c = ((2.443315711809948e-5 * z - 1.388731625493765e-3) * z + 4.166664568298827e-2) * z * z - 0.5 * z + 1.0
    quarter = turn.astype(jnp.int32)
    odd = (quarter & 1) == 1
    sine = jnp.where(odd, c, s)
    cosine = jnp.where(odd, s, c)
    sine = jnp.where((quarter & 2) == 2, -sine, sine)
    cosine = jnp.where(((quarter + 1) & 2) == 2, -cosine, cosine)
    return sine, cosine


def kernel(
    nlat, nlon,
    route, tblk, depth, fric, mask, forc, ocell, otime, oval, oweight,
    x_out, r_out,
    dw, dwn, dws, dwe, dww, wetb, wetfric, coef, diag,
    payf, payi, outf, outi, inf, ini, plan, splan, mats, oslot,
    d, db, x, r, q, hd, hx, hr, hq, pk, sum_a, sum_b, send_b,
    hs, hrv, as_, ar, bs, br, os_, orv, ds_, dr, loc,
):
    rows, cols = depth.shape
    nblk = cols // BLOCK
    slots = nlon * CAP
    tiles = otime.shape[0]
    me_lat = lax.axis_index("lat")
    me_lon = lax.axis_index("lon")
    north, south = lax.rem(me_lat + 1, nlat), lax.rem(me_lat + nlat - 1, nlat)
    east, west = lax.rem(me_lon + 1, nlon), lax.rem(me_lon + nlon - 1, nlon)

    barrier = pltpu.get_barrier_semaphore()
    for k in range(1, nlon):
        pl.semaphore_signal(barrier, inc=1, device_id={"lon": lax.rem(me_lon + k, nlon)}, device_id_type=MESH)
    for k in range(1, nlat):
        pl.semaphore_signal(barrier, inc=1, device_id={"lat": lax.rem(me_lat + k, nlat)}, device_id_type=MESH)

    def remote(src, dst, send, recv, where):
        return pltpu.make_async_remote_copy(
            src_ref=src, dst_ref=dst, send_sem=send, recv_sem=recv, device_id=where, device_id_type=MESH
        )

    lane = lax.broadcasted_iota(jnp.int32, (1, BLOCK), 1)
    lane8 = lax.broadcasted_iota(jnp.int32, (8, BLOCK), 1)
    sub8 = lax.broadcasted_iota(jnp.int32, (8, BLOCK), 0)

    wet = mask[...].astype(jnp.float32)
    dw[...] = depth[...] * wet

    for t in range(tiles):
        payf[t, 0:1] = otime[t : t + 1]
        payf[t, 1:2] = oval[t : t + 1]
        payf[t, 2:3] = oweight[t : t + 1]
        payf[t, 3:4] = jnp.zeros((1, BLOCK), jnp.float32)
        payi[t] = jnp.broadcast_to(ocell[t : t + 1] + tblk[t] * BLOCK, (8, BLOCK))
    payf[tiles] = jnp.zeros((8, BLOCK), jnp.float32)
    payi[tiles] = jnp.zeros((8, BLOCK), jnp.int32)

    def pick(p, carry):
        first, second = jnp.int32(tiles), jnp.int32(tiles)
        for t in reversed(range(tiles)):
            hit = route[t, 0] == p
            second = jnp.where(hit, first, second)
            first = jnp.where(hit, jnp.int32(t), first)
        one, two = payf[first], payf[second]
        outf[p] = jnp.concatenate([one[0:4], two[0:4]], axis=0)
        outi[p] = jnp.where(sub8 == 0, payi[first], payi[second])
        return carry

    lax.fori_loop(0, nlon, pick, 0)
    pl.semaphore_wait(barrier, nlon + nlat - 2)

    first_copies = [
        remote(dw, dws, ds_.at[0], dr.at[0], {"lat": north}),
        remote(dw, dwn, ds_.at[1], dr.at[1], {"lat": south}),
        remote(dw.at[:, pl.ds(0, BLOCK)], dwe, ds_.at[2], dr.at[2], {"lon": west}),
        remote(dw.at[:, pl.ds(cols - BLOCK, BLOCK)], dww, ds_.at[3], dr.at[3], {"lon": east}),
    ]

    def obs_copy(k):
        peer = lax.rem(me_lon + k, nlon)
        return [
            remote(outf.at[peer], inf.at[me_lon], os_.at[0, peer], orv.at[0, me_lon], {"lon": peer}),
            remote(outi.at[peer], ini.at[me_lon], os_.at[1, peer], orv.at[1, me_lon], {"lon": peer}),
        ]

    def obs_wait(k):
        peer = lax.rem(me_lon + k, nlon)
        remote(outf.at[peer], inf.at[peer], os_.at[0, peer], orv.at[0, peer], {"lon": peer}).wait_recv()
        remote(outi.at[peer], ini.at[peer], os_.at[1, peer], orv.at[1, peer], {"lon": peer}).wait_recv()

    obs_sends = [c for k in range(1, nlon) for c in obs_copy(k)]
    for c in obs_sends:
        c.start()
    for c in first_copies:
        c.start()
    inf[me_lon] = outf[me_lon]
    ini[me_lon] = outi[me_lon]

    for cb in range(nblk):
        at = pl.ds(cb * BLOCK, BLOCK)
        for h in range(2):
            r[pl.ds(1, rows), h, :, at] = jnp.swapaxes(forc[h, :, :, at], 0, 1)
    x[...] = jnp.zeros_like(x)
    hx[...] = jnp.zeros_like(hx)
    oslot[slots] = jnp.zeros((2, 8, BLOCK), jnp.float32)

    for c in first_copies:
        c.wait_recv()
    a = dw[...]
    colid = lax.broadcasted_iota(jnp.int32, (rows, cols), 1)
    rowid = lax.broadcasted_iota(jnp.int32, (rows, cols), 0)
    keep_n = (me_lat < nlat - 1).astype(jnp.float32)
    keep_s = (me_lat > 0).astype(jnp.float32)

    def harmonic(first, second):
        return 2.0 * first * second / jnp.maximum(first + second, 0.5)

    side = harmonic(a, jnp.where(colid == cols - 1, dwe[:, 0:1], pltpu.roll(a, cols - 1, 1)))
    total = side
    for row in range(rows):
        coef[0, row] = jnp.broadcast_to(side[row : row + 1], (8, cols))
    side = harmonic(a, jnp.where(colid == 0, dww[:, BLOCK - 1 : BLOCK], pltpu.roll(a, 1, 1)))
    total = total + side
    for row in range(rows):
        coef[1, row] = jnp.broadcast_to(side[row : row + 1], (8, cols))
    side = harmonic(a, jnp.where(rowid == rows - 1, dwn[0:1, :] * keep_n, pltpu.roll(a, rows - 1, 0)))
    total = total + side
    for row in range(rows):
        coef[2, row] = jnp.broadcast_to(side[row : row + 1], (8, cols))
    side = harmonic(a, jnp.where(rowid == 0, dws[rows - 1 : rows, :] * keep_s, pltpu.roll(a, 1, 0)))
    total = total + side
    for row in range(rows):
        coef[3, row] = jnp.broadcast_to(side[row : row + 1], (8, cols))
    stiff = jnp.zeros((8, 1), jnp.float32)
    rate = jnp.zeros((8, BLOCK), jnp.float32)
    sub1 = lax.broadcasted_iota(jnp.int32, (8, 1), 0)
    for c in range(8):
        stiff = jnp.where(sub1 == c, float(STIFF[c]), stiff)
        rate = jnp.where(sub8 == c, float(RATES[c]), rate)
    drag = fric[...]
    total = total + wet * drag + (1.0 - wet)
    for row in range(rows):
        wide = jnp.broadcast_to(wet[row : row + 1], (8, cols))
        wetb[row] = wide
        wetfric[row] = wide * jnp.broadcast_to(drag[row : row + 1], (8, cols))
        diag[row] = wide * stiff + jnp.broadcast_to(total[row : row + 1], (8, cols))

    for k in range(1, nlon):
        obs_wait(k)
    rep = jnp.full((1, BLOCK), slots, jnp.int32)
    homes = jnp.full((1, BLOCK), -1, jnp.int32)
    for s in reversed(range(slots)):
        home = ini[s // CAP, pl.ds(s % CAP, 1), :] >> 7
        rep = jnp.where(home == lane, s, rep)
        homes = jnp.where(lane == s, home, homes)
    chain = jnp.full((1, BLOCK), slots, jnp.int32)
    for s in reversed(range(slots)):
        home = ini[s // CAP, pl.ds(s % CAP, 1), :] >> 7
        chain = jnp.where((home == homes) & (lane < s), s, chain)
    plan[...] = jnp.where(
        sub8 == 0,
        jnp.broadcast_to(homes, (8, BLOCK)),
        jnp.where(sub8 == 1, jnp.broadcast_to(chain, (8, BLOCK)), jnp.broadcast_to(rep, (8, BLOCK))),
    )
    to_scalars = pltpu.make_async_copy(plan, splan, loc.at[0])
    to_scalars.start()

    cells = lax.broadcasted_iota(jnp.int32, (BLOCK, BLOCK), 0)

    def build(o, carry):
        for k in range(CAP):
            times = inf[o, pl.ds(4 * k, 1), :]
            value = inf[o, pl.ds(4 * k + 1, 1), :]
            weight = inf[o, pl.ds(4 * k + 2, 1), :]
            cell = ini[o, pl.ds(k, 1), :] & (BLOCK - 1)
            sine, cosine = sin_cos(rate * times)
            basis = (cosine, sine)
            weighted = (weight * cosine, weight * sine)
            parts = []
            for h in range(2):
                for c in range(8):
                    one = weighted[h][c : c + 1]
                    parts.append(one * basis[0])
                    parts.append(one * basis[1])
            parts.append(weighted[0] * value)
            parts.append(weighted[1] * value)
            terms = jnp.concatenate(parts, axis=0)
            high = terms.astype(jnp.bfloat16)
            low = (terms - high.astype(jnp.float32)).astype(jnp.bfloat16)
            hot = (cells == cell).astype(jnp.float32).astype(jnp.bfloat16)
            mats[o * CAP + k] = lax.dot_general(
                jnp.concatenate([high, low], axis=1),
                jnp.concatenate([hot, hot], axis=1),
                (((1,), (1,)), ((), ())),
                preferred_element_type=jnp.float32,
            )
        return carry

    lax.fori_loop(0, nlon, build, 0)
    to_scalars.wait()

    def first_slots(i, carry):
        s = slots - 1 - i
        after = oslot[splan[1, s]]
        oslot[s] = mats[s, 256:272, :].reshape(2, 8, BLOCK) + after
        return carry

    lax.fori_loop(0, slots, first_slots, 0)

    def pack(row, col, value, packed):
        shift = row if col == 0 else row + 1
        moved = pltpu.roll(value, shift, 2)
        return jnp.where(lane8 == row, moved, packed)

    zero = jnp.zeros((2, 8, BLOCK), jnp.float32)

    def start_rhs(row, carry):
        lo, hi = carry
        for cb in range(nblk):
            at = pl.ds(cb * BLOCK, BLOCK)
            v = wetb[row, :, at] * r[row + 1, :, :, at] + oslot[splan[2, row * nblk + cb]]
            r[row + 1, :, :, at] = v
            q[STEPS, row + 1, :, :, at] = v
            db[(row + 1) * nblk + cb] = v
            if cb == 0:
                lo = pack(row, 0, v, lo)
            if cb == nblk - 1:
                hi = pack(row, 1, v, hi)
        return lo, hi

    lo, hi = lax.fori_loop(0, rows, start_rhs, (zero, zero))
    pk[STEPS, 0] = lo
    pk[STEPS, 1] = hi

    def halo(i):
        return [
            remote(q.at[i, 1], q.at[i, rows + 1], hs.at[i, 0], hrv.at[i, 0], {"lat": south}),
            remote(q.at[i, rows], q.at[i, 0], hs.at[i, 1], hrv.at[i, 1], {"lat": north}),
            remote(pk.at[i, 0], hq.at[i, 1], hs.at[i, 2], hrv.at[i, 2], {"lon": west}),
            remote(pk.at[i, 1], hq.at[i, 0], hs.at[i, 3], hrv.at[i, 3], {"lon": east}),
        ]

    def begin(i):
        for c in halo(i):
            c.start()
        d[pl.ds(1, rows)] = r[pl.ds(1, rows)]
        for c in halo(i):
            c.wait()
        for edge in (0, rows + 1):
            d[edge] = q[i, edge]
            r[edge] = q[i, edge]
        hd[...] = hq[i]
        hr[...] = hq[i]

    def all_sum(i, part):
        sum_a[i, me_lat] = part
        for k in range(1, nlat):
            peer = lax.rem(me_lat + k, nlat)
            remote(sum_a.at[i, me_lat], sum_a.at[i, me_lat], as_.at[i, peer], ar.at[i, me_lat], {"lat": peer}).start()
        for k in range(1, nlat):
            peer = lax.rem(me_lat + k, nlat)
            remote(sum_a.at[i, peer], sum_a.at[i, peer], as_.at[i, peer], ar.at[i, peer], {"lat": peer}).wait_recv()
        part = sum_a[i, 0]
        for k in range(1, nlat):
            part = part + sum_a[i, k]
        sum_b[i, me_lon] = part
        for k in range(1, nlon):
            peer = lax.rem(me_lon + k, nlon)
            remote(sum_b.at[i, me_lon], sum_b.at[i, me_lon], bs.at[i, peer], br.at[i, me_lon], {"lon": peer}).start()
        for k in range(1, nlon):
            peer = lax.rem(me_lon + k, nlon)
            remote(sum_b.at[i, peer], sum_b.at[i, peer], bs.at[i, peer], br.at[i, peer], {"lon": peer}).wait_recv()
        part = sum_b[i, 0]
        for k in range(1, nlon):
            part = part + sum_b[i, k]
        return jnp.sum(part, axis=1, keepdims=True)

    def sides(ref, halos, row):
        v = [ref[row + 1, :, :, pl.ds(cb * BLOCK, BLOCK)] for cb in range(nblk)]
        to_west = [pltpu.roll(b, BLOCK - 1, 2) for b in v]
        to_west.append(pltpu.roll(halos[1], BLOCK - 1 - row, 2))
        to_east = [pltpu.roll(halos[0], BLOCK - row, 2)] + [pltpu.roll(b, 1, 2) for b in v]
        e = [jnp.where(lane8 == BLOCK - 1, to_west[cb + 1], to_west[cb]) for cb in range(nblk)]
        w = [jnp.where(lane8 == 0, to_east[cb], to_east[cb + 1]) for cb in range(nblk)]
        return v, e, w

    def step(i, carry):
        def slot(j, carry):
            s = slots - 1 - j
            after = oslot[splan[1, s]]
            v = db[splan[0, s] + nblk]
            acc = [after, zero]
            for c in range(16):
                m = mats[s, 16 * c : 16 * c + 16, :].reshape(2, 8, BLOCK)
                acc[c % 2] = acc[c % 2] + m * v[c // 8, c % 8 : c % 8 + 1, :]
            oslot[s] = acc[0] + acc[1]
            return carry

        lax.fori_loop(0, slots, slot, 0)

        def line(row, carry):
            lo, hi, rr, rq, dq, qq = carry
            v, e, w = sides(d, hd, row)
            for cb in range(nblk):
                at = pl.ds(cb * BLOCK, BLOCK)
                image = (
                    diag[row, :, at] * v[cb]
                    - coef[0, row, :, at] * e[cb]
                    - coef[1, row, :, at] * w[cb]
                    - coef[2, row, :, at] * d[row + 2, :, :, at]
                    - coef[3, row, :, at] * d[row, :, :, at]
                    + oslot[splan[2, row * nblk + cb]]
                )
                q[i, row + 1, :, :, at] = image
                res = r[row + 1, :, :, at]
                rr = rr + res * res
                rq = rq + res * image
                dq = dq + v[cb] * image
                qq = qq + image * image
                if cb == 0:
                    lo = pack(row, 0, image, lo)
                if cb == nblk - 1:
                    hi = pack(row, 1, image, hi)
            return lo, hi, rr, rq, dq, qq

        lo, hi, *sums = lax.fori_loop(0, rows, line, (zero,) * 6)
        pk[i, 0] = lo
        pk[i, 1] = hi
        part = jnp.zeros((8, BLOCK), jnp.float32)
        for k, s in enumerate(sums):
            part = jnp.where(sub8 == k, jnp.sum(s[0] + s[1], axis=0, keepdims=True), part)
        for c in halo(i):
            c.start()
        whole = all_sum(i, part)
        rr, rq, dq, qq = (whole[k : k + 1] for k in range(4))
        size = rr / dq
        beta = (rr - 2.0 * size * rq + size * size * qq) / rr
        for c in halo(i):
            c.wait()

        def update(row, carry):
            for cb in range(nblk):
                at = pl.ds(cb * BLOCK, BLOCK)
                old = d[row, :, :, at]
                x[row, :, :, at] = x[row, :, :, at] + size * old
                res = r[row, :, :, at] - size * q[i, row, :, :, at]
                r[row, :, :, at] = res
                new = res + beta * old
                d[row, :, :, at] = new
                db[row * nblk + cb] = new
            return carry

        lax.fori_loop(0, rows + 2, update, 0)
        hx[...] = hx[...] + size * hd[...]
        hr[...] = hr[...] - size * hq[i]
        hd[...] = hr[...] + beta * hd[...]
        for k in range(1, nlat):
            peer = lax.rem(me_lat + k, nlat)
            remote(sum_a.at[i, me_lat], sum_a.at[i, me_lat], as_.at[i, peer], ar.at[i, me_lat], {"lat": peer}).wait_send()
        for k in range(1, nlon):
            peer = lax.rem(me_lon + k, nlon)
            remote(sum_b.at[i, me_lon], sum_b.at[i, me_lon], bs.at[i, peer], br.at[i, me_lon], {"lon": peer}).wait_send()
        return carry

    begin(STEPS)
    for c in obs_sends + first_copies:
        c.wait_send()
    lax.fori_loop(0, ITERS, step, 0)

    def friction(row, carry):
        lo, hi = carry
        v, e, _ = sides(x, hx, row)
        for cb in range(nblk):
            at = pl.ds(cb * BLOCK, BLOCK)
            flux_e = coef[0, row, :, at] * (e[cb] - v[cb])
            flux_n = coef[2, row, :, at] * (x[row + 2, :, :, at] - v[cb])
            square = flux_e * flux_e + flux_n * flux_n
            speed = jnp.sum(square[0] + square[1], axis=0, keepdims=True)
            extra = wetfric[row, :, at] * (jnp.sqrt(1.0 + speed / 16.0) - 1.0)
            diag[row, :, at] = diag[row, :, at] + extra
            res = r[row + 1, :, :, at] - extra * v[cb]
            r[row + 1, :, :, at] = res
            q[STEPS + 1, row + 1, :, :, at] = res
            db[(row + 1) * nblk + cb] = res
            if cb == 0:
                lo = pack(row, 0, res, lo)
            if cb == nblk - 1:
                hi = pack(row, 1, res, hi)
        return lo, hi

    lo, hi = lax.fori_loop(0, rows, friction, (zero, zero))
    pk[STEPS + 1, 0] = lo
    pk[STEPS + 1, 1] = hi
    begin(STEPS + 1)
    lax.fori_loop(ITERS, STEPS, step, 0)

    for cb in range(nblk):
        at = pl.ds(cb * BLOCK, BLOCK)
        for h in range(2):
            x_out[h, :, :, at] = jnp.swapaxes(x[pl.ds(1, rows), h, :, at], 0, 1)
            r_out[h, :, :, at] = jnp.swapaxes(r[pl.ds(1, rows), h, :, at], 0, 1)


def shards(nlat, nlon, depth, friction, ocean_mask, forcing, tile_route, tile_block, obs_cell, obs_time, obs_value, obs_weight):
    channels, rows, cols = forcing.shape
    slots = nlon * CAP
    nblk, tiles = cols // BLOCK, obs_time.shape[0]
    f32, i32 = jnp.float32, jnp.int32
    vmem = pl.BlockSpec(memory_space=pltpu.VMEM)
    smem = pl.BlockSpec(memory_space=pltpu.SMEM)
    field = (rows + 2, 2, 8, cols)
    dma = pltpu.SemaphoreType.DMA
    scratch = [
        pltpu.VMEM((rows, cols), f32),
        pltpu.VMEM((rows, cols), f32),
        pltpu.VMEM((rows, cols), f32),
        pltpu.VMEM((rows, BLOCK), f32),
        pltpu.VMEM((rows, BLOCK), f32),
        pltpu.VMEM((rows, 8, cols), f32),
        pltpu.VMEM((rows, 8, cols), f32),
        pltpu.VMEM((4, rows, 8, cols), f32),
        pltpu.VMEM((rows, 8, cols), f32),
        pltpu.VMEM((tiles + 1, 8, BLOCK), f32),
        pltpu.VMEM((tiles + 1, 8, BLOCK), i32),
        pltpu.VMEM((nlon, 8, BLOCK), f32),
        pltpu.VMEM((nlon, 8, BLOCK), i32),
        pltpu.VMEM((nlon, 8, BLOCK), f32),
        pltpu.VMEM((nlon, 8, BLOCK), i32),
        pltpu.VMEM((8, BLOCK), i32),
        pltpu.SMEM((8, BLOCK), i32),
        pltpu.VMEM((slots, 272, BLOCK), f32),
        pltpu.VMEM((slots + 1, 2, 8, BLOCK), f32),
        pltpu.VMEM(field, f32),
        pltpu.VMEM(((rows + 2) * nblk, 2, 8, BLOCK), f32),
        pltpu.VMEM(field, f32),
        pltpu.VMEM(field, f32),
        pltpu.VMEM((STEPS + 2,) + field, f32),
        pltpu.VMEM((2, 2, 8, BLOCK), f32),
        pltpu.VMEM((2, 2, 8, BLOCK), f32),
        pltpu.VMEM((2, 2, 8, BLOCK), f32),
        pltpu.VMEM((STEPS + 2, 2, 2, 8, BLOCK), f32),
        pltpu.VMEM((STEPS + 2, 2, 2, 8, BLOCK), f32),
        pltpu.VMEM((STEPS, nlat, 8, BLOCK), f32),
        pltpu.VMEM((STEPS, nlon, 8, BLOCK), f32),
        pltpu.VMEM((8, BLOCK), f32),
        dma((STEPS + 2, 4)),
        dma((STEPS + 2, 4)),
        dma((STEPS, nlat)),
        dma((STEPS, nlat)),
        dma((STEPS, nlon)),
        dma((STEPS, nlon)),
        dma((2, nlon)),
        dma((2, nlon)),
        dma((4,)),
        dma((4,)),
        dma((1,)),
    ]
    shape = jax.ShapeDtypeStruct((2, channels // 2, rows, cols), f32)
    x, r = pl.pallas_call(
        functools.partial(kernel, nlat, nlon),
        out_shape=(shape, shape),
        in_specs=[smem, smem] + [vmem] * 8,
        out_specs=(vmem, vmem),
        scratch_shapes=scratch,
        compiler_params=pltpu.CompilerParams(
            collective_id=0, has_side_effects=True, vmem_limit_bytes=40 * 2**20
        ),
    )(
        tile_route, tile_block, depth, friction, ocean_mask, forcing.reshape(2, channels // 2, rows, cols),
        obs_cell, obs_time, obs_value, obs_weight,
    )
    return x.reshape(forcing.shape), r.reshape(forcing.shape)


def solution(mesh):
    tile = P(("lat", "lon"), None)
    grid = P("lat", "lon")
    in_specs = (grid, grid, grid, P(None, "lat", "lon"), tile, P(("lat", "lon")), tile, tile, tile, tile)
    out_specs = (P(None, "lat", "lon"), P(None, "lat", "lon"))
    body = functools.partial(shards, mesh.shape["lat"], mesh.shape["lon"])
    return jax.shard_map(body, mesh=mesh, in_specs=in_specs, out_specs=out_specs, check_vma=False)
```

```python
import functools
import math

import jax
import jax.numpy as jnp
import numpy as np
from jax import lax
from jax.experimental import pallas as pl
from jax.experimental.pallas import tpu as pltpu
from jax.sharding import PartitionSpec as P

BLOCK = 128
CAP = 2
ITERS = 3
OUTER = 2
STEPS = ITERS * OUTER
MESH = pl.DeviceIdType.MESH
OMEGA_DEGREES = (28.984104, 30.0, 28.43973, 30.082137, 15.041069, 13.943036, 14.958931, 13.398661)
RATES = np.array(OMEGA_DEGREES, np.float32) * np.float32(math.pi / 180.0)
STIFF = np.float32(0.2) * (RATES / RATES[0]) ** 2


def sin_cos(angle):
    turn = jnp.floor(angle * (2.0 / math.pi) + 0.5)
    x = ((angle - turn * 1.5703125) - turn * 4.837512969970703125e-4) - turn * 7.54978995489188216e-8
    z = x * x
    s = ((-1.9515295891e-4 * z + 8.3321608736e-3) * z - 1.6666654611e-1) * z * x + x
    c = ((2.443315711809948e-5 * z - 1.388731625493765e-3) * z + 4.166664568298827e-2) * z * z - 0.5 * z + 1.0
    quarter = turn.astype(jnp.int32)
    odd = (quarter & 1) == 1
    sine = jnp.where(odd, c, s)
    cosine = jnp.where(odd, s, c)
    sine = jnp.where((quarter & 2) == 2, -sine, sine)
    cosine = jnp.where(((quarter + 1) & 2) == 2, -cosine, cosine)
    return sine, cosine


def kernel(
    nlat, nlon,
    route, tblk, *refs,
):
    sources, refs = refs[:8], refs[8:]
    landed = refs[-9:-1]
    work(nlat, nlon, sources, refs[-1], route, tblk, *landed, *refs[:-9])


def work(
    nlat, nlon, sources, load,
    route, tblk, depth, fric, mask, forc, ocell, otime, oval, oweight,
    x_out, r_out,
    dw, dwn, dws, dwe, dww, wetb, wetfric, coef, diag,
    payf, payi, outf, outi, inf, ini, plan, splan, mats, oslot,
    d, db, x, r, q, hd, hx, hr, hq, pk, sum_a, sum_b, send_b,
    hs, hrv, as_, ar, bs, br, os_, orv, ds_, dr, loc,
):
    rows, cols = depth.shape
    nblk = cols // BLOCK
    slots = nlon * CAP
    tiles = otime.shape[0]
    me_lat = lax.axis_index("lat")
    me_lon = lax.axis_index("lon")
    north, south = lax.rem(me_lat + 1, nlat), lax.rem(me_lat + nlat - 1, nlat)
    east, west = lax.rem(me_lon + 1, nlon), lax.rem(me_lon + nlon - 1, nlon)

    loads = [
        pltpu.make_async_copy(src, dst, load.at[k])
        for k, (src, dst) in enumerate(zip(sources, (depth, fric, mask, forc, ocell, otime, oval, oweight)))
    ]
    for c in loads:
        c.start()
    barrier = pltpu.get_barrier_semaphore()
    for k in range(1, nlon):
        pl.semaphore_signal(barrier, inc=1, device_id={"lon": lax.rem(me_lon + k, nlon)}, device_id_type=MESH)
    for k in range(1, nlat):
        pl.semaphore_signal(barrier, inc=1, device_id={"lat": lax.rem(me_lat + k, nlat)}, device_id_type=MESH)

    def remote(src, dst, send, recv, where):
        return pltpu.make_async_remote_copy(
            src_ref=src, dst_ref=dst, send_sem=send, recv_sem=recv, device_id=where, device_id_type=MESH
        )

    lane = lax.broadcasted_iota(jnp.int32, (1, BLOCK), 1)
    lane8 = lax.broadcasted_iota(jnp.int32, (8, BLOCK), 1)
    sub8 = lax.broadcasted_iota(jnp.int32, (8, BLOCK), 0)

    for c in loads:
        c.wait()
    wet = mask[...].astype(jnp.float32)
    dw[...] = depth[...] * wet

    for t in range(tiles):
        payf[t, 0:1] = otime[t : t + 1]
        payf[t, 1:2] = oval[t : t + 1]
        payf[t, 2:3] = oweight[t : t + 1]
        payf[t, 3:4] = jnp.zeros((1, BLOCK), jnp.float32)
        payi[t] = jnp.broadcast_to(ocell[t : t + 1] + tblk[t] * BLOCK, (8, BLOCK))
    payf[tiles] = jnp.zeros((8, BLOCK), jnp.float32)
    payi[tiles] = jnp.zeros((8, BLOCK), jnp.int32)

    def pick(p, carry):
        first, second = jnp.int32(tiles), jnp.int32(tiles)
        for t in reversed(range(tiles)):
            hit = route[t, 0] == p
            second = jnp.where(hit, first, second)
            first = jnp.where(hit, jnp.int32(t), first)
        one, two = payf[first], payf[second]
        outf[p] = jnp.concatenate([one[0:4], two[0:4]], axis=0)
        outi[p] = jnp.where(sub8 == 0, payi[first], payi[second])
        return carry

    lax.fori_loop(0, nlon, pick, 0)
    pl.semaphore_wait(barrier, nlon + nlat - 2)

    first_copies = [
        remote(dw, dws, ds_.at[0], dr.at[0], {"lat": north}),
        remote(dw, dwn, ds_.at[1], dr.at[1], {"lat": south}),
        remote(dw.at[:, pl.ds(0, BLOCK)], dwe, ds_.at[2], dr.at[2], {"lon": west}),
        remote(dw.at[:, pl.ds(cols - BLOCK, BLOCK)], dww, ds_.at[3], dr.at[3], {"lon": east}),
    ]

    def obs_copy(k):
        peer = lax.rem(me_lon + k, nlon)
        return [
            remote(outf.at[peer], inf.at[me_lon], os_.at[0, peer], orv.at[0, me_lon], {"lon": peer}),
            remote(outi.at[peer], ini.at[me_lon], os_.at[1, peer], orv.at[1, me_lon], {"lon": peer}),
        ]

    def obs_wait(k):
        peer = lax.rem(me_lon + k, nlon)
        remote(outf.at[peer], inf.at[peer], os_.at[0, peer], orv.at[0, peer], {"lon": peer}).wait_recv()
        remote(outi.at[peer], ini.at[peer], os_.at[1, peer], orv.at[1, peer], {"lon": peer}).wait_recv()

    obs_sends = [c for k in range(1, nlon) for c in obs_copy(k)]
    for c in obs_sends:
        c.start()
    for c in first_copies:
        c.start()
    inf[me_lon] = outf[me_lon]
    ini[me_lon] = outi[me_lon]

    for cb in range(nblk):
        at = pl.ds(cb * BLOCK, BLOCK)
        for h in range(2):
            r[pl.ds(1, rows), h, :, at] = jnp.swapaxes(forc[h, :, :, at], 0, 1)
    x[...] = jnp.zeros_like(x)
    hx[...] = jnp.zeros_like(hx)
    oslot[slots] = jnp.zeros((2, 8, BLOCK), jnp.float32)

    for c in first_copies:
        c.wait_recv()
    a = dw[...]
    colid = lax.broadcasted_iota(jnp.int32, (rows, cols), 1)
    rowid = lax.broadcasted_iota(jnp.int32, (rows, cols), 0)
    keep_n = (me_lat < nlat - 1).astype(jnp.float32)
    keep_s = (me_lat > 0).astype(jnp.float32)

    def harmonic(first, second):
        return 2.0 * first * second / jnp.maximum(first + second, 0.5)

    side = harmonic(a, jnp.where(colid == cols - 1, dwe[:, 0:1], pltpu.roll(a, cols - 1, 1)))
    total = side
    for row in range(rows):
        coef[0, row] = jnp.broadcast_to(side[row : row + 1], (8, cols))
    side = harmonic(a, jnp.where(colid == 0, dww[:, BLOCK - 1 : BLOCK], pltpu.roll(a, 1, 1)))
    total = total + side
    for row in range(rows):
        coef[1, row] = jnp.broadcast_to(side[row : row + 1], (8, cols))
    side = harmonic(a, jnp.where(rowid == rows - 1, dwn[0:1, :] * keep_n, pltpu.roll(a, rows - 1, 0)))
    total = total + side
    for row in range(rows):
        coef[2, row] = jnp.broadcast_to(side[row : row + 1], (8, cols))
    side = harmonic(a, jnp.where(rowid == 0, dws[rows - 1 : rows, :] * keep_s, pltpu.roll(a, 1, 0)))
    total = total + side
    for row in range(rows):
        coef[3, row] = jnp.broadcast_to(side[row : row + 1], (8, cols))
    stiff = jnp.zeros((8, 1), jnp.float32)
    rate = jnp.zeros((8, BLOCK), jnp.float32)
    sub1 = lax.broadcasted_iota(jnp.int32, (8, 1), 0)
    for c in range(8):
        stiff = jnp.where(sub1 == c, float(STIFF[c]), stiff)
        rate = jnp.where(sub8 == c, float(RATES[c]), rate)
    drag = fric[...]
    total = total + wet * drag + (1.0 - wet)
    for row in range(rows):
        wide = jnp.broadcast_to(wet[row : row + 1], (8, cols))
        wetb[row] = wide
        wetfric[row] = wide * jnp.broadcast_to(drag[row : row + 1], (8, cols))
        diag[row] = wide * stiff + jnp.broadcast_to(total[row : row + 1], (8, cols))

    for k in range(1, nlon):
        obs_wait(k)
    rep = jnp.full((1, BLOCK), slots, jnp.int32)
    homes = jnp.full((1, BLOCK), -1, jnp.int32)
    for s in reversed(range(slots)):
        home = ini[s // CAP, pl.ds(s % CAP, 1), :] >> 7
        rep = jnp.where(home == lane, s, rep)
        homes = jnp.where(lane == s, home, homes)
    chain = jnp.full((1, BLOCK), slots, jnp.int32)
    for s in reversed(range(slots)):
        home = ini[s // CAP, pl.ds(s % CAP, 1), :] >> 7
        chain = jnp.where((home == homes) & (lane < s), s, chain)
    plan[...] = jnp.where(
        sub8 == 0,
        jnp.broadcast_to(homes, (8, BLOCK)),
        jnp.where(sub8 == 1, jnp.broadcast_to(chain, (8, BLOCK)), jnp.broadcast_to(rep, (8, BLOCK))),
    )
    to_scalars = pltpu.make_async_copy(plan, splan, loc.at[0])
    to_scalars.start()

    cells = lax.broadcasted_iota(jnp.int32, (BLOCK, BLOCK), 0)

    def build(o, carry):
        for k in range(CAP):
            times = inf[o, pl.ds(4 * k, 1), :]
            value = inf[o, pl.ds(4 * k + 1, 1), :]
            weight = inf[o, pl.ds(4 * k + 2, 1), :]
            cell = ini[o, pl.ds(k, 1), :] & (BLOCK - 1)
            sine, cosine = sin_cos(rate * times)
            basis = (cosine, sine)
            weighted = (weight * cosine, weight * sine)
            parts = []
            for h in range(2):
                for c in range(8):
                    one = weighted[h][c : c + 1]
                    parts.append(one * basis[0])
                    parts.append(one * basis[1])
            parts.append(weighted[0] * value)
            parts.append(weighted[1] * value)
            terms = jnp.concatenate(parts, axis=0)
            high = terms.astype(jnp.bfloat16)
            low = (terms - high.astype(jnp.float32)).astype(jnp.bfloat16)
            hot = (cells == cell).astype(jnp.float32).astype(jnp.bfloat16)
            mats[o * CAP + k] = lax.dot_general(
                jnp.concatenate([high, low], axis=1),
                jnp.concatenate([hot, hot], axis=1),
                (((1,), (1,)), ((), ())),
                preferred_element_type=jnp.float32,
            )
        return carry

    lax.fori_loop(0, nlon, build, 0)
    to_scalars.wait()

    def first_slots(i, carry):
        s = slots - 1 - i
        after = oslot[splan[1, s]]
        oslot[s] = mats[s, 256:272, :].reshape(2, 8, BLOCK) + after
        return carry

    lax.fori_loop(0, slots, first_slots, 0)

    def pack(row, col, value, packed):
        shift = row if col == 0 else row + 1
        moved = pltpu.roll(value, shift, 2)
        return jnp.where(lane8 == row, moved, packed)

    zero = jnp.zeros((2, 8, BLOCK), jnp.float32)

    def start_rhs(row, carry):
        lo, hi = carry
        for cb in range(nblk):
            at = pl.ds(cb * BLOCK, BLOCK)
            v = wetb[row, :, at] * r[row + 1, :, :, at] + oslot[splan[2, row * nblk + cb]]
            r[row + 1, :, :, at] = v
            q[STEPS, row + 1, :, :, at] = v
            db[(row + 1) * nblk + cb] = v
            if cb == 0:
                lo = pack(row, 0, v, lo)
            if cb == nblk - 1:
                hi = pack(row, 1, v, hi)
        return lo, hi

    lo, hi = lax.fori_loop(0, rows, start_rhs, (zero, zero))
    pk[STEPS, 0] = lo
    pk[STEPS, 1] = hi

    def halo(i):
        return [
            remote(q.at[i, 1], q.at[i, rows + 1], hs.at[i, 0], hrv.at[i, 0], {"lat": south}),
            remote(q.at[i, rows], q.at[i, 0], hs.at[i, 1], hrv.at[i, 1], {"lat": north}),
            remote(pk.at[i, 0], hq.at[i, 1], hs.at[i, 2], hrv.at[i, 2], {"lon": west}),
            remote(pk.at[i, 1], hq.at[i, 0], hs.at[i, 3], hrv.at[i, 3], {"lon": east}),
        ]

    def begin(i):
        for c in halo(i):
            c.start()
        d[pl.ds(1, rows)] = r[pl.ds(1, rows)]
        for c in halo(i):
            c.wait()
        for edge in (0, rows + 1):
            d[edge] = q[i, edge]
            r[edge] = q[i, edge]
        hd[...] = hq[i]
        hr[...] = hq[i]

    def all_sum(i, part):
        sum_a[i, me_lat] = part
        for k in range(1, nlat):
            peer = lax.rem(me_lat + k, nlat)
            remote(sum_a.at[i, me_lat], sum_a.at[i, me_lat], as_.at[i, peer], ar.at[i, me_lat], {"lat": peer}).start()
        for k in range(1, nlat):
            peer = lax.rem(me_lat + k, nlat)
            remote(sum_a.at[i, peer], sum_a.at[i, peer], as_.at[i, peer], ar.at[i, peer], {"lat": peer}).wait_recv()
        part = sum_a[i, 0]
        for k in range(1, nlat):
            part = part + sum_a[i, k]
        sum_b[i, me_lon] = part
        for k in range(1, nlon):
            peer = lax.rem(me_lon + k, nlon)
            remote(sum_b.at[i, me_lon], sum_b.at[i, me_lon], bs.at[i, peer], br.at[i, me_lon], {"lon": peer}).start()
        for k in range(1, nlon):
            peer = lax.rem(me_lon + k, nlon)
            remote(sum_b.at[i, peer], sum_b.at[i, peer], bs.at[i, peer], br.at[i, peer], {"lon": peer}).wait_recv()
        part = sum_b[i, 0]
        for k in range(1, nlon):
            part = part + sum_b[i, k]
        return jnp.sum(part, axis=1, keepdims=True)

    def sides(ref, halos, row):
        v = [ref[row + 1, :, :, pl.ds(cb * BLOCK, BLOCK)] for cb in range(nblk)]
        to_west = [pltpu.roll(b, BLOCK - 1, 2) for b in v]
        to_west.append(pltpu.roll(halos[1], BLOCK - 1 - row, 2))
        to_east = [pltpu.roll(halos[0], BLOCK - row, 2)] + [pltpu.roll(b, 1, 2) for b in v]
        e = [jnp.where(lane8 == BLOCK - 1, to_west[cb + 1], to_west[cb]) for cb in range(nblk)]
        w = [jnp.where(lane8 == 0, to_east[cb], to_east[cb + 1]) for cb in range(nblk)]
        return v, e, w

    def step(i, carry):
        def slot(j, carry):
            s = slots - 1 - j
            after = oslot[splan[1, s]]
            v = db[splan[0, s] + nblk]
            acc = [after, zero]
            for c in range(16):
                m = mats[s, 16 * c : 16 * c + 16, :].reshape(2, 8, BLOCK)
                acc[c % 2] = acc[c % 2] + m * v[c // 8, c % 8 : c % 8 + 1, :]
            oslot[s] = acc[0] + acc[1]
            return carry

        lax.fori_loop(0, slots, slot, 0)

        def line(row, carry):
            lo, hi, rr, rq, dq, qq = carry
            v, e, w = sides(d, hd, row)
            for cb in range(nblk):
                at = pl.ds(cb * BLOCK, BLOCK)
                image = (
                    diag[row, :, at] * v[cb]
                    - coef[0, row, :, at] * e[cb]
                    - coef[1, row, :, at] * w[cb]
                    - coef[2, row, :, at] * d[row + 2, :, :, at]
                    - coef[3, row, :, at] * d[row, :, :, at]
                    + oslot[splan[2, row * nblk + cb]]
                )
                q[i, row + 1, :, :, at] = image
                res = r[row + 1, :, :, at]
                rr = rr + res * res
                rq = rq + res * image
                dq = dq + v[cb] * image
                qq = qq + image * image
                if cb == 0:
                    lo = pack(row, 0, image, lo)
                if cb == nblk - 1:
                    hi = pack(row, 1, image, hi)
            return lo, hi, rr, rq, dq, qq

        lo, hi, *sums = lax.fori_loop(0, rows, line, (zero,) * 6)
        pk[i, 0] = lo
        pk[i, 1] = hi
        part = jnp.zeros((8, BLOCK), jnp.float32)
        for k, s in enumerate(sums):
            part = jnp.where(sub8 == k, jnp.sum(s[0] + s[1], axis=0, keepdims=True), part)
        more = lax.rem(i, ITERS) < ITERS - 1

        @pl.when(more)
        def _():
            for c in halo(i):
                c.start()

        whole = all_sum(i, part)
        rr, rq, dq, qq = (whole[k : k + 1] for k in range(4))
        size = rr / dq
        beta = (rr - 2.0 * size * rq + size * size * qq) / rr

        @pl.when(more)
        def _():
            for c in halo(i):
                c.wait()

        def update(row, carry):
            for cb in range(nblk):
                at = pl.ds(cb * BLOCK, BLOCK)
                old = d[row, :, :, at]
                x[row, :, :, at] = x[row, :, :, at] + size * old
                res = r[row, :, :, at] - size * q[i, row, :, :, at]
                r[row, :, :, at] = res
                new = res + beta * old
                d[row, :, :, at] = new
                db[row * nblk + cb] = new
            return carry

        lax.fori_loop(0, rows + 2, update, 0)
        hx[...] = hx[...] + size * hd[...]
        hr[...] = hr[...] - size * hq[i]
        hd[...] = hr[...] + beta * hd[...]
        for k in range(1, nlat):
            peer = lax.rem(me_lat + k, nlat)
            remote(sum_a.at[i, me_lat], sum_a.at[i, me_lat], as_.at[i, peer], ar.at[i, me_lat], {"lat": peer}).wait_send()
        for k in range(1, nlon):
            peer = lax.rem(me_lon + k, nlon)
            remote(sum_b.at[i, me_lon], sum_b.at[i, me_lon], bs.at[i, peer], br.at[i, me_lon], {"lon": peer}).wait_send()
        return carry

    begin(STEPS)
    for c in obs_sends + first_copies:
        c.wait_send()
    lax.fori_loop(0, ITERS, step, 0)

    def friction(row, carry):
        lo, hi = carry
        v, e, _ = sides(x, hx, row)
        for cb in range(nblk):
            at = pl.ds(cb * BLOCK, BLOCK)
            flux_e = coef[0, row, :, at] * (e[cb] - v[cb])
            flux_n = coef[2, row, :, at] * (x[row + 2, :, :, at] - v[cb])
            square = flux_e * flux_e + flux_n * flux_n
            speed = jnp.sum(square[0] + square[1], axis=0, keepdims=True)
            extra = wetfric[row, :, at] * (jnp.sqrt(1.0 + speed / 16.0) - 1.0)
            diag[row, :, at] = diag[row, :, at] + extra
            res = r[row + 1, :, :, at] - extra * v[cb]
            r[row + 1, :, :, at] = res
            q[STEPS + 1, row + 1, :, :, at] = res
            db[(row + 1) * nblk + cb] = res
            if cb == 0:
                lo = pack(row, 0, res, lo)
            if cb == nblk - 1:
                hi = pack(row, 1, res, hi)
        return lo, hi

    lo, hi = lax.fori_loop(0, rows, friction, (zero, zero))
    pk[STEPS + 1, 0] = lo
    pk[STEPS + 1, 1] = hi
    begin(STEPS + 1)
    lax.fori_loop(ITERS, STEPS, step, 0)

    for cb in range(nblk):
        at = pl.ds(cb * BLOCK, BLOCK)
        for h in range(2):
            x_out[h, :, :, at] = jnp.swapaxes(x[pl.ds(1, rows), h, :, at], 0, 1)
            r_out[h, :, :, at] = jnp.swapaxes(r[pl.ds(1, rows), h, :, at], 0, 1)


def shards(nlat, nlon, depth, friction, ocean_mask, forcing, tile_route, tile_block, obs_cell, obs_time, obs_value, obs_weight):
    channels, rows, cols = forcing.shape
    slots = nlon * CAP
    nblk, tiles = cols // BLOCK, obs_time.shape[0]
    f32, i32 = jnp.float32, jnp.int32
    vmem = pl.BlockSpec(memory_space=pltpu.VMEM)
    smem = pl.BlockSpec(memory_space=pltpu.SMEM)
    field = (rows + 2, 2, 8, cols)
    dma = pltpu.SemaphoreType.DMA
    scratch = [
        pltpu.VMEM((rows, cols), f32),
        pltpu.VMEM((rows, cols), f32),
        pltpu.VMEM((rows, cols), f32),
        pltpu.VMEM((rows, BLOCK), f32),
        pltpu.VMEM((rows, BLOCK), f32),
        pltpu.VMEM((rows, 8, cols), f32),
        pltpu.VMEM((rows, 8, cols), f32),
        pltpu.VMEM((4, rows, 8, cols), f32),
        pltpu.VMEM((rows, 8, cols), f32),
        pltpu.VMEM((tiles + 1, 8, BLOCK), f32),
        pltpu.VMEM((tiles + 1, 8, BLOCK), i32),
        pltpu.VMEM((nlon, 8, BLOCK), f32),
        pltpu.VMEM((nlon, 8, BLOCK), i32),
        pltpu.VMEM((nlon, 8, BLOCK), f32),
        pltpu.VMEM((nlon, 8, BLOCK), i32),
        pltpu.VMEM((8, BLOCK), i32),
        pltpu.SMEM((8, BLOCK), i32),
        pltpu.VMEM((slots, 272, BLOCK), f32),
        pltpu.VMEM((slots + 1, 2, 8, BLOCK), f32),
        pltpu.VMEM(field, f32),
        pltpu.VMEM(((rows + 2) * nblk, 2, 8, BLOCK), f32),
        pltpu.VMEM(field, f32),
        pltpu.VMEM(field, f32),
        pltpu.VMEM((STEPS + 2,) + field, f32),
        pltpu.VMEM((2, 2, 8, BLOCK), f32),
        pltpu.VMEM((2, 2, 8, BLOCK), f32),
        pltpu.VMEM((2, 2, 8, BLOCK), f32),
        pltpu.VMEM((STEPS + 2, 2, 2, 8, BLOCK), f32),
        pltpu.VMEM((STEPS + 2, 2, 2, 8, BLOCK), f32),
        pltpu.VMEM((STEPS, nlat, 8, BLOCK), f32),
        pltpu.VMEM((STEPS, nlon, 8, BLOCK), f32),
        pltpu.VMEM((8, BLOCK), f32),
        dma((STEPS + 2, 4)),
        dma((STEPS + 2, 4)),
        dma((STEPS, nlat)),
        dma((STEPS, nlat)),
        dma((STEPS, nlon)),
        dma((STEPS, nlon)),
        dma((2, nlon)),
        dma((2, nlon)),
        dma((4,)),
        dma((4,)),
        dma((1,)),
        pltpu.VMEM((rows, cols), f32),
        pltpu.VMEM((rows, cols), f32),
        pltpu.VMEM((rows, cols), i32),
        pltpu.VMEM((2, channels // 2, rows, cols), f32),
        pltpu.VMEM((tiles, BLOCK), i32),
        pltpu.VMEM((tiles, BLOCK), f32),
        pltpu.VMEM((tiles, BLOCK), f32),
        pltpu.VMEM((tiles, BLOCK), f32),
        dma((8,)),
    ]
    shape = jax.ShapeDtypeStruct((2, channels // 2, rows, cols), f32)
    x, r = pl.pallas_call(
        functools.partial(kernel, nlat, nlon),
        out_shape=(shape, shape),
        in_specs=[smem, smem] + [pl.BlockSpec(memory_space=pltpu.HBM)] * 8,
        out_specs=(vmem, vmem),
        scratch_shapes=scratch,
        compiler_params=pltpu.CompilerParams(
            collective_id=0, has_side_effects=True, vmem_limit_bytes=40 * 2**20
        ),
    )(
        tile_route, tile_block, depth, friction, ocean_mask, forcing.reshape(2, channels // 2, rows, cols),
        obs_cell, obs_time, obs_value, obs_weight,
    )
    return x.reshape(forcing.shape), r.reshape(forcing.shape)


def solution(mesh):
    tile = P(("lat", "lon"), None)
    grid = P("lat", "lon")
    in_specs = (grid, grid, grid, P(None, "lat", "lon"), tile, P(("lat", "lon")), tile, tile, tile, tile)
    out_specs = (P(None, "lat", "lon"), P(None, "lat", "lon"))
    body = functools.partial(shards, mesh.shape["lat"], mesh.shape["lon"])
    return jax.shard_map(body, mesh=mesh, in_specs=in_specs, out_specs=out_specs, check_vma=False)
```
